32 devices in a mesh: dp: 8 (over y, x, core), blk: 4 (over z).
Axes of the slice: x: 2, y: 2, z: 4, core: 2. Of those that a mesh axis runs over, the one named last changes fastest.
Arguments:
- clip_embed: bfloat16 [4096, 1152], P(('dp', 'blk')), may hold values from -0.1875 to 0.1875
- caption_embed: bfloat16 [4096, 1152], P(('dp', 'blk')), may hold values from -0.1875 to 0.1875
- positive: int32 [4096], P(('dp', 'blk')), may hold values from 0 to 4095, each once
Outputs:
- clip_grad: float32 [4096, 1152], P(('dp', 'blk'))
- caption_grad: float32 [4096, 1152], P(('dp', 'blk'))
- row_loss: float32 [4096], P(('dp', 'blk'))
The draws below stay inside these ranges and needn't reach their ends.
Inputs may be any that keep to these rules, and one draw needn't show every extreme that they name: `positive`: each caption is paired with exactly one clip.
All inputs are finite; a program needn't handle non-finite values.
Results may differ from the reference program's by a relative error of at most 0.0031.
Values may be sent and summed in bfloat16 or wider, within the bound.
A program may use at most 128 MiB of HBM per device.

```python
import jax
import jax.numpy as jnp
from jax import lax

D = 1152
PAIRS = 4096


def shard_levels(rng, shape, shards, low, high):
    factor_of = 1.0
    for dim, shards_of in shards:
        heights = jax.random.uniform(jax.random.fold_in(jax.random.fold_in(rng, 6), dim), (shards_of,), jnp.float32, low / len(shards), high / len(shards))
        factor_of = factor_of * jnp.repeat(jnp.exp(heights), shape[dim] // shards_of).reshape((-1,) + (1,) * (len(shape) - 1 - dim))
    return factor_of


def bell_draw(stream_key, extent, spread, limit, shards=(), kind=jnp.bfloat16):
    result = spread * jax.random.normal(stream_key, extent, jnp.float32)
    if shards:
        result = result * shard_levels(stream_key, extent, shards, -0.22, 0.18)
    return jnp.clip(result, -limit, limit).astype(kind)


def setup_inputs(seed: int = 0) -> dict:
    arg_keys = jax.random.split(jax.random.key(seed), 4)
    clip_embed = bell_draw(arg_keys[0], (PAIRS, D), D ** -0.5, 0.1875, ((0, 32),))
    caption_embed = bell_draw(arg_keys[1], (PAIRS, D), D ** -0.5, 0.1875, ((0, 32),))
    positive = jax.random.permutation(arg_keys[2], PAIRS).astype(jnp.int32)
    return {"clip_embed": clip_embed, "caption_embed": caption_embed, "positive": positive}


TEMP = 30.0
BIAS = -8.0
EPS = 1e-06

def unit_rows(embed):
    values = embed.astype(jnp.float32)
    scale = jnp.sqrt(lax.optimization_barrier(jnp.sum(values * values, axis=1, keepdims=True)) + EPS)
    return (values / scale, scale)

def pull_back(unit_f, scale, grad_unit):
    inner = lax.optimization_barrier(jnp.sum(unit_f * grad_unit, axis=1, keepdims=True))
    return (grad_unit - unit_f * inner) / scale

def reference(clip_embed, caption_embed, positive):
    clip_unit, clip_scale = unit_rows(clip_embed)
    caption_unit, caption_scale = unit_rows(caption_embed)
    clip_low = lax.optimization_barrier(clip_unit.astype(jnp.bfloat16)).astype(jnp.float32)
    caption_low = lax.optimization_barrier(caption_unit.astype(jnp.bfloat16)).astype(jnp.float32)
    block = min(PAIRS, 1024)
    count = PAIRS // block
    col_ids = jnp.arange(PAIRS, dtype=jnp.int32)

    def one_block(carry, index):
        start = (index * block).astype(jnp.int32)
        rows = lax.dynamic_slice_in_dim(clip_low, start, block, 0)
        row_pos = lax.dynamic_slice_in_dim(positive, start, block, 0)
        logits = TEMP * jnp.dot(rows, caption_low.T, precision=lax.Precision.HIGHEST) + BIAS
        sign = jnp.where(row_pos[:, None] == col_ids[None, :], 1.0, -1.0).astype(jnp.float32)
        loss_rows = lax.optimization_barrier(jnp.sum(jax.nn.softplus(-sign * logits), axis=1))
        slope = -sign * jax.nn.sigmoid(-sign * logits)
        slope = lax.optimization_barrier(slope.astype(jnp.bfloat16)).astype(jnp.float32)
        grad_rows = TEMP * jnp.dot(slope, caption_low, precision=lax.Precision.HIGHEST)
        carry = carry + TEMP * jnp.dot(slope.T, rows, precision=lax.Precision.HIGHEST)
        return (carry, (grad_rows, loss_rows))
    start_acc = jnp.zeros((PAIRS, D), jnp.float32)
    caption_unit_grad, (grad_blocks, loss_blocks) = lax.scan(one_block, start_acc, jnp.arange(count, dtype=jnp.int32))
    clip_unit_grad = grad_blocks.reshape(PAIRS, D)
    row_loss = loss_blocks.reshape(PAIRS)
    clip_grad = pull_back(clip_unit, clip_scale, clip_unit_grad)
    caption_grad = pull_back(caption_unit, caption_scale, caption_unit_grad)
    return (clip_grad, caption_grad, row_loss)
```

```python
import functools

import jax
import jax.numpy as jnp
from jax import lax
from jax.experimental import pallas as pl
from jax.experimental.pallas import tpu as pltpu
from jax.sharding import PartitionSpec as P

TEMP = 30.0
BIAS = -8.0
EPS = 1e-06
MESH = pl.DeviceIdType.MESH
BF = jnp.bfloat16
F32 = jnp.float32


def unit_rows(embed):
    values = embed.astype(F32)
    scale = jnp.sqrt(jnp.sum(values * values, axis=1, keepdims=True) + EPS)
    return values / scale, scale


def pull_back(embed, grad_unit):
    unit_f, scale = unit_rows(embed)
    inner = jnp.sum(unit_f * grad_unit, axis=1, keepdims=True)
    return (grad_unit - unit_f * inner) / scale


def kernel(Y, X, NZ, clip_ref, cap_ref, pos_ref, clip_out, cap_out, loss_out,
           clips, caps, capown, pos, pt, loss, capacc, xsend, xrecv, zsend, zrecv,
           csend, crecv, lcrecv, yacc, ysend, yrecv, lyrecv, zcsend, zcrecv, lzrecv,
           ssem, clip_r, pos_r, cap_r, x_r, z_r, c_r, y_r, zc_r, l_r):
    R, D = clip_ref.shape
    dp = lax.axis_index("dp")
    z = lax.axis_index("blk")
    c = dp % 2
    x = (dp // 2) % X
    y = dp // (2 * X)
    sib = 1 - c
    zr = z % 2
    zo = 1 - zr
    zc = z + 1 - 2 * zr

    def dev(yy, xx, cc, zz):
        return ((yy * X + xx) * 2 + cc, zz)

    def rows(slot, n=1):
        return pl.ds(pl.multiple_of(slot * R, R), n * R)

    def slot_of(cc, yy, k):
        return (cc * Y + yy) * 2 + k

    count = [0]
    sent = []

    def send(src, dst, rsem, where, cond=None):
        copy = pltpu.make_async_remote_copy(
            src_ref=src, dst_ref=dst, send_sem=ssem.at[count[0]], recv_sem=rsem,
            device_id=where, device_id_type=MESH)
        count[0] += 1
        sent.append((copy, cond))
        if cond is None:
            copy.start()
        else:
            pl.when(cond)(copy.start)

    def arrive(dst, rsem):
        pltpu.make_async_remote_copy(
            src_ref=dst, dst_ref=dst, send_sem=ssem.at[0], recv_sem=rsem,
            device_id=dev(y, x, sib, z), device_id_type=MESH).wait_recv()

    ys = [(y + d) % Y for d in range(1, Y)]
    xs = [(x + d) % X for d in range(1, X)]
    peers = [dev(y, x, c, (z + d) % NZ) for d in range(1, NZ)]
    peers += [dev(yy, x, c, z) for yy in ys] + [dev(y, xx, c, z) for xx in xs]
    peers += [dev(y, x, sib, z)]
    barrier = pltpu.get_barrier_semaphore()
    for peer in peers:
        pl.semaphore_signal(barrier, inc=1, device_id=peer, device_id_type=MESH)

    mine = slot_of(c, y, zr)
    other = slot_of(c, y, zo)
    clips[rows(mine), :] = unit_rows(clip_ref[...])[0].astype(BF)
    capown[...] = unit_rows(cap_ref[...])[0].astype(BF)
    pos[c, y, zr] = pos_ref[0]
    pl.semaphore_wait(barrier, len(peers))

    send(clips.at[rows(mine)], clips.at[rows(mine)], clip_r.at[mine], dev(y, x, c, zc))
    send(pos.at[c, y, zr], pos.at[c, y, zr], pos_r.at[0], dev(y, x, c, zc))
    for j in range(2):
        to = z // 2 + 2 * j
        slot = zr * X + x
        send(capown, caps.at[rows(slot)], cap_r.at[slot], dev(y, x, c, to), to != z)
    for yy in ys:
        send(clips.at[rows(mine)], clips.at[rows(mine)], clip_r.at[mine], dev(yy, x, c, z))
    send(clips.at[rows(mine)], clips.at[rows(mine)], clip_r.at[mine], dev(y, x, sib, z))
    for k in range(2):
        w = 2 * zr + k
        slot = k * X + x

        @pl.when(w == z)
        def _():
            caps[rows(slot), :] = capown[...]

        for xx in xs:
            send(caps.at[rows(slot)], caps.at[rows(slot)], cap_r.at[slot], dev(y, xx, c, z), w == z)
    arrive(clips.at[rows(other)], clip_r.at[other])
    for yy in ys:
        send(clips.at[rows(other)], clips.at[rows(other)], clip_r.at[other], dev(yy, x, c, z))
    send(clips.at[rows(other)], clips.at[rows(other)], clip_r.at[other], dev(y, x, sib, z))
    arrive(pos.at[c, y, zo], pos_r.at[0])
    for yy in ys:
        send(pos.at[c, y], pos.at[c, y], pos_r.at[1 + y], dev(yy, x, c, z))
    for k in range(2):
        w = 2 * zr + k
        slot = k * X + x

        @pl.when(w != z)
        def _():
            arrive(caps.at[rows(slot)], cap_r.at[slot])

        for xx in xs:
            send(caps.at[rows(slot)], caps.at[rows(slot)], cap_r.at[slot], dev(y, xx, c, z), w != z)
    for k in (zr, zo):
        for yy in ys:
            slot = slot_of(c, yy, k)
            arrive(clips.at[rows(slot)], clip_r.at[slot])
            send(clips.at[rows(slot)], clips.at[rows(slot)], clip_r.at[slot], dev(y, x, sib, z))
    for yy in ys:
        arrive(pos.at[c, yy], pos_r.at[1 + yy])
    send(pos.at[c], pos.at[c], pos_r.at[1 + Y], dev(y, x, sib, z))
    for k in range(2):
        for xx in xs:
            slot = k * X + xx
            arrive(caps.at[rows(slot)], cap_r.at[slot])
    for yy in range(Y):
        for k in range(2):
            slot = slot_of(sib, yy, k)
            arrive(clips.at[rows(slot)], clip_r.at[slot])
    arrive(pos.at[sib], pos_r.at[1 + Y])

    half = X * R
    tile = lax.broadcasted_iota(jnp.int32, (half, 1), 0)
    cap_dev = (y * X + tile // R) * 2 + c

    def scores(i, _):
        k = i // (2 * Y)
        b = i % (2 * Y)
        cc = b // Y
        yy = b % Y
        cols = pl.ds(pl.multiple_of(b * 2 * R, 2 * R), 2 * R)
        sel = pl.ds(pl.multiple_of(k * half, half), half)
        dots = lax.dot_general(caps[sel, :], clips[cols, :], (((1,), (1,)), ((), ())),
                               preferred_element_type=F32)
        logits = TEMP * dots + BIAS
        ids = (cap_dev * NZ + 2 * zr + k) * R + tile % R
        both = pos[cc, yy]
        target = jnp.concatenate([both[0], both[1]], axis=1)
        hit = ids == target
        t = jnp.where(hit, -logits, logits)
        a = jnp.exp(-jnp.abs(t))
        soft = jnp.maximum(t, 0.0) + jnp.log1p(a)
        sig = jnp.where(t >= 0.0, 1.0, a) / (1.0 + a)
        pt[sel, cols] = jnp.where(hit, -sig, sig).astype(BF)
        part = jnp.sum(soft, axis=0, keepdims=True)
        for m in range(2):
            old = jnp.where(k == 0, 0.0, loss[cc, yy, m])
            loss[cc, yy, m] = old + part[:, m * R:(m + 1) * R]
        return 0

    loss[...] = jnp.zeros_like(loss)
    lax.fori_loop(0, 4 * Y, scores, 0)
    send(loss.at[sib], lcrecv, l_r.at[0], dev(y, x, sib, z))

    def clip_part(cc, yy):
        cols = pl.ds(pl.multiple_of((cc * Y + yy) * 2 * R, 2 * R), 2 * R)
        return TEMP * lax.dot_general(pt[:, cols], caps[...], (((0,), (0,)), ((), ())),
                                      preferred_element_type=F32)

    for yy in ys + [y]:
        csend[yy] = clip_part(sib, yy).astype(BF)
        send(csend.at[yy], crecv.at[yy], c_r.at[yy], dev(y, x, sib, z))

    for k in range(2):
        for xx in xs + [x]:
            slot = k * X + xx
            g = TEMP * jnp.dot(pt[rows(slot), :], clips[...], preferred_element_type=F32)
            if xx is x:
                capacc[k] = g
            else:
                xsend[slot] = g.astype(BF)
                send(xsend.at[slot], xrecv.at[k * X + x], x_r.at[k * X + x], dev(y, xx, c, z))

    arrive(lcrecv, l_r.at[0])
    loss[c] = loss[c] + lcrecv[...]
    for yy in ys:
        send(loss.at[c, yy], lyrecv.at[y], l_r.at[1 + y], dev(yy, x, c, z))
    for yy in ys:
        g = clip_part(c, yy)
        arrive(crecv.at[yy], c_r.at[yy])
        ysend[yy] = (g + crecv[yy].astype(F32)).astype(BF)
        for k in (zo, zr):
            send(ysend.at[yy, rows(k)], yrecv.at[y, rows(k)], y_r.at[y, k], dev(yy, x, c, z))
    g = clip_part(c, y)
    arrive(crecv.at[y], c_r.at[y])
    yacc[...] = g + crecv[y].astype(F32)

    for k in range(2):
        w = 2 * zr + k
        for xx in xs:
            arrive(xrecv.at[k * X + xx], x_r.at[k * X + xx])
            capacc[k] = capacc[k] + xrecv[k * X + xx].astype(F32)
        zsend[k] = capacc[k].astype(BF)
        send(zsend.at[k], zrecv.at[z // 2], z_r.at[z // 2], dev(y, x, c, w), w != z)

    for yy in ys:
        arrive(lyrecv.at[yy], l_r.at[1 + yy])
        loss[c, y] = loss[c, y] + lyrecv[yy]
    send(loss.at[c, y, zo], lzrecv, l_r.at[1 + Y], dev(y, x, c, zc))
    for yy in ys:
        arrive(yrecv.at[yy, rows(zo)], y_r.at[yy, zo])
        yacc[rows(zo), :] = yacc[rows(zo), :] + yrecv[yy, rows(zo), :].astype(F32)
    zcsend[...] = yacc[rows(zo), :].astype(BF)
    send(zcsend, zcrecv, zc_r.at[0], dev(y, x, c, zc))
    for yy in ys:
        arrive(yrecv.at[yy, rows(zr)], y_r.at[yy, zr])
        yacc[rows(zr), :] = yacc[rows(zr), :] + yrecv[yy, rows(zr), :].astype(F32)

    arrive(lzrecv, l_r.at[1 + Y])
    loss_out[...] = loss[c, y, zr] + lzrecv[...]
    cap_out[...] = jnp.zeros_like(cap_out)
    for j in range(2):
        p = z // 2 + 2 * j

        @pl.when(p == z)
        def _():
            cap_out[...] = cap_out[...] + capacc[z % 2]

        @pl.when(p != z)
        def _():
            arrive(zrecv.at[j], z_r.at[j])
            cap_out[...] = cap_out[...] + zrecv[j].astype(F32)

    cap_out[...] = pull_back(cap_ref[...], cap_out[...])
    arrive(zcrecv, zc_r.at[0])
    clip_out[...] = pull_back(clip_ref[...], yacc[rows(zr), :] + zcrecv[...].astype(F32))

    for copy, cond in sent:
        if cond is None:
            copy.wait_send()
        else:
            pl.when(cond)(copy.wait_send)


def local(Y, X, NZ, clip_embed, caption_embed, positive):
    R, D = clip_embed.shape
    ncl, ncap = 4 * Y, 2 * X
    V = pltpu.VMEM
    dma = pltpu.SemaphoreType.DMA
    scratch = [
        V((ncl * R, D), BF), V((ncap * R, D), BF), V((R, D), BF),
        V((2, Y, 2, 1, R), jnp.int32), V((ncap * R, ncl * R), BF), V((2, Y, 2, 1, R), F32),
        V((2, R, D), F32), V((ncap, R, D), BF), V((ncap, R, D), BF), V((2, R, D), BF), V((2, R, D), BF),
        V((Y, 2 * R, D), BF), V((Y, 2 * R, D), BF), V((Y, 2, 1, R), F32),
        V((2 * R, D), F32), V((Y, 2 * R, D), BF), V((Y, 2 * R, D), BF), V((Y, 2, 1, R), F32),
        V((R, D), BF), V((R, D), BF), V((1, R), F32),
        dma((16 + 12 * (X + Y),)), dma((ncl,)), dma((2 + Y,)), dma((ncap,)), dma((ncap,)), dma((2,)),
        dma((Y,)), dma((Y, 2)), dma((1,)), dma((2 + Y,)),
    ]
    vm = pl.BlockSpec(memory_space=V)
    clip_grad, cap_grad, loss = pl.pallas_call(
        functools.partial(kernel, Y, X, NZ),
        out_shape=(jax.ShapeDtypeStruct((R, D), F32), jax.ShapeDtypeStruct((R, D), F32),
                   jax.ShapeDtypeStruct((1, R), F32)),
        in_specs=[vm] * 3, out_specs=(vm,) * 3, scratch_shapes=scratch,
        compiler_params=pltpu.CompilerParams(
            collective_id=0, has_side_effects=True, vmem_limit_bytes=56 * 1024 * 1024),
    )(clip_embed, caption_embed, positive.reshape(1, 1, R))
    return clip_grad, cap_grad, loss.reshape(R)


def solution(mesh):
    n_dp, n_blk = mesh.shape["dp"], mesh.shape["blk"]
    assert n_blk == 4 and n_dp % 2 == 0
    plane = n_dp // 2
    Y = max(d for d in range(1, plane + 1) if plane % d == 0 and d * d <= plane)
    X = plane // Y
    specs = (P(("dp", "blk"), None), P(("dp", "blk"), None), P(("dp", "blk")))
    return jax.shard_map(functools.partial(local, Y, X, n_blk), mesh=mesh, in_specs=specs,
                         out_specs=specs, check_vma=False)
```

```python
import functools

import jax
import jax.numpy as jnp
from jax import lax
from jax.experimental import pallas as pl
from jax.experimental.pallas import tpu as pltpu
from jax.sharding import PartitionSpec as P

TEMP = 30.0
BIAS = -8.0
EPS = 1e-06
MESH = pl.DeviceIdType.MESH
BF = jnp.bfloat16
F32 = jnp.float32
NG = 4
NP = 2
WS = 2


def unit_rows(embed):
    values = embed.astype(F32)
    scale = jnp.sqrt(jnp.sum(values * values, axis=1, keepdims=True) + EPS)
    return values / scale, scale


def pull_back(embed, grad_unit):
    unit_f, scale = unit_rows(embed)
    inner = jnp.sum(unit_f * grad_unit, axis=1, keepdims=True)
    return (grad_unit - unit_f * inner) / scale


def kernel(Y, X, NZ, clip_ref, cap_ref, pos_ref, clip_out, cap_out, loss_out,
           clips, caps, capown, pos, pt, loss, capacc, xsend, xrecv, zsend, zrecv,
           csend, crecv, lcrecv, acc, yacc, ysend, yrecv, lyrecv, zcsend, zcrecv, lzrecv,
           ssem, clip_r, pos_r, cap_r, x_r, z_r, c_r, y_r, zc_r, l_r):
    R, D = clip_ref.shape
    H, HG = R // NP, R // NG
    dp = lax.axis_index("dp")
    z = lax.axis_index("blk")
    c = dp % 2
    x = (dp // 2) % X
    y = dp // (2 * X)
    sib = 1 - c
    zr = z % 2
    zo = 1 - zr
    zc = z + 1 - 2 * zr

    def dev(yy, xx, cc, zz):
        return ((yy * X + xx) * 2 + cc, zz)

    def rows(slot, n=1):
        return pl.ds(pl.multiple_of(slot * R, R), n * R)

    def piece(slot, p):
        return pl.ds(pl.multiple_of(slot * R + p * HG, HG), HG)

    def slot_of(cc, yy, k):
        return (k * Y + yy) * 2 + cc

    count = [0]
    sent = []

    def send(src, dst, rsem, where, cond=None):
        copy = pltpu.make_async_remote_copy(
            src_ref=src, dst_ref=dst, send_sem=ssem.at[count[0]], recv_sem=rsem,
            device_id=where, device_id_type=MESH)
        count[0] += 1
        sent.append((copy, cond))
        if cond is None:
            copy.start()
        else:
            pl.when(cond)(copy.start)

    done = set()

    def settle(first, last=None):
        for i in range(first, len(sent) if last is None else last):
            if i in done:
                continue
            done.add(i)
            copy, cond = sent[i]
            if cond is None:
                copy.wait_send()
            else:
                pl.when(cond)(copy.wait_send)

    def arrive(dst, rsem):
        pltpu.make_async_remote_copy(
            src_ref=dst, dst_ref=dst, send_sem=ssem.at[0], recv_sem=rsem,
            device_id=dev(y, x, sib, z), device_id_type=MESH).wait_recv()

    ys = [(y + d) % Y for d in range(1, Y)]
    xs = [(x + d) % X for d in range(1, X)]
    peers = [dev(y, x, c, (z + d) % NZ) for d in range(1, NZ)]
    peers += [dev(yy, x, c, z) for yy in ys] + [dev(y, xx, c, z) for xx in xs]
    peers += [dev(y, x, sib, z)]
    barrier = pltpu.get_barrier_semaphore()
    for peer in peers:
        pl.semaphore_signal(barrier, inc=1, device_id=peer, device_id_type=MESH)

    mine = slot_of(c, y, zr)
    other = slot_of(c, y, zo)
    clips[rows(mine), :] = unit_rows(clip_ref[...])[0].astype(BF)
    capown[...] = unit_rows(cap_ref[...])[0].astype(BF)
    pos[c, y, zr] = pos_ref[0]
    pl.semaphore_wait(barrier, len(peers))

    owner = 3 * zr == z
    passer = jnp.logical_not(owner)
    for p in range(NG):
        part = clips.at[piece(mine, p)]
        send(part, part, clip_r.at[mine, p], dev(y, x, c, zc))
        for j in range(2):
            to = z // 2 + 2 * j
            slot = zr * X + x
            send(capown.at[pl.ds(p * HG, HG)], caps.at[piece(slot, p)], cap_r.at[slot, p],
                 dev(y, x, c, to), to != z)
    send(pos.at[c, y, zr], pos.at[c, y, zr], pos_r.at[0], dev(y, x, c, zc))
    whole = clips.at[rows(mine)]
    for yy in ys:
        send(whole, whole, clip_r.at[mine, 0], dev(yy, x, c, z))
    send(whole, whole, clip_r.at[mine, 0], dev(y, x, sib, z))
    near, far = zr * X + x, zo * X + x

    @pl.when(owner)
    def _():
        caps[rows(near), :] = capown[...]

    for p in range(NG):
        part = caps.at[piece(near, p)]
        for xx in xs:
            send(part, part, cap_r.at[near, p], dev(y, xx, c, z), owner)
    for p in range(NG):
        part = clips.at[piece(other, p)]
        arrive(part, clip_r.at[other, p])
        for yy in ys:
            send(part, part, clip_r.at[other, p], dev(yy, x, c, z))
        part = caps.at[piece(far, p)]
        arrive(part, cap_r.at[far, p])
        for xx in xs:
            send(part, part, cap_r.at[far, p], dev(y, xx, c, z))
        part = caps.at[piece(near, p)]

        @pl.when(passer)
        def _():
            arrive(part, cap_r.at[near, p])

        for xx in xs:
            send(part, part, cap_r.at[near, p], dev(y, xx, c, z), passer)
    whole = clips.at[rows(other)]
    send(whole, whole, clip_r.at[other, 0], dev(y, x, sib, z))
    arrive(pos.at[c, y, zo], pos_r.at[0])
    for yy in ys:
        send(pos.at[c, y], pos.at[c, y], pos_r.at[1 + y], dev(yy, x, c, z))
    for yy in ys:
        slot = slot_of(c, yy, zr)
        whole = clips.at[rows(slot)]
        arrive(whole, clip_r.at[slot, 0])
        send(whole, whole, clip_r.at[slot, 0], dev(y, x, sib, z))
    for yy in ys:
        arrive(pos.at[c, yy], pos_r.at[1 + yy])
    send(pos.at[c], pos.at[c], pos_r.at[1 + Y], dev(y, x, sib, z))
    for yy in ys:
        slot = slot_of(c, yy, zo)
        for p in range(NG):
            arrive(clips.at[piece(slot, p)], clip_r.at[slot, p])
        whole = clips.at[rows(slot)]
        send(whole, whole, clip_r.at[slot, 0], dev(y, x, sib, z))
    for k in range(2):
        for xx in xs:
            slot = k * X + xx
            for p in range(NG):
                arrive(caps.at[piece(slot, p)], cap_r.at[slot, p])
    for yy in range(Y):
        for k in range(2):
            slot = slot_of(sib, yy, k)
            arrive(clips.at[rows(slot)], clip_r.at[slot, 0])
    arrive(pos.at[sib], pos_r.at[1 + Y])

    half = X * R
    tile = lax.broadcasted_iota(jnp.int32, (half, 1), 0)
    cap_dev = (y * X + tile // R) * 2 + c

    def scores(k, kk, yy):
        b = kk * Y + yy
        cols = pl.ds(pl.multiple_of(b * 2 * R, 2 * R), 2 * R)
        sel = pl.ds(pl.multiple_of(k * half, half), half)
        dots = lax.dot_general(caps[sel, :], clips[cols, :], (((1,), (1,)), ((), ())),
                               preferred_element_type=F32)
        logits = TEMP * dots + BIAS
        ids = (cap_dev * NZ + 2 * zr + k) * R + tile % R
        target = jnp.concatenate([pos[0, yy, kk], pos[1, yy, kk]], axis=1)
        hit = ids == target
        t = jnp.where(hit, -logits, logits)
        a = jnp.exp(-jnp.abs(t))
        soft = jnp.maximum(t, 0.0) + jnp.log1p(a)
        sig = jnp.where(t >= 0.0, 1.0, a) / (1.0 + a)
        pt[sel, cols] = jnp.where(hit, -sig, sig).astype(BF)
        part = jnp.sum(soft, axis=0, keepdims=True)
        for m in range(2):
            loss[m, yy, kk] = loss[m, yy, kk] + part[:, m * R:(m + 1) * R]

    loss[...] = jnp.zeros_like(loss)

    def cap_part(k, xx):
        return TEMP * jnp.dot(pt[rows(k * X + xx), :], clips[...], preferred_element_type=F32)

    def clip_part(k, yy):
        both = pl.ds(pl.multiple_of((k * Y + yy) * 2 * R, 2 * R), 2 * R)
        acc[...] = TEMP * lax.dot_general(pt[:, both], caps[...], (((0,), (0,)), ((), ())),
                                          preferred_element_type=F32)
        csend[k, yy] = acc[rows(sib), :].astype(BF)
        send(csend.at[k, yy], crecv.at[k, yy], c_r.at[k, yy], dev(y, x, sib, z))
        yacc[k, yy] = acc[rows(c), :]

    def clip_both(k, yy):
        arrive(crecv.at[k, yy], c_r.at[k, yy])
        return yacc[k, yy] + crecv[k, yy].astype(F32)

    def cap_on(k, p, cond):
        part = pl.ds(p * H, H)
        g = capacc[k, part]
        for xx in xs:
            arrive(xrecv.at[k * X + xx, part], x_r.at[k * X + xx, p])
            g = g + xrecv[k * X + xx, part].astype(F32)
        capacc[k, part] = g
        zsend[k, part] = g.astype(BF)
        send(zsend.at[k, part], zrecv.at[z // 2, part], z_r.at[z // 2, p], dev(y, x, c, 2 * zr + k), cond)

    def clip_own(k, p):
        part = pl.ds(p * H, H)
        g = yacc[k, y, part]
        for yy in ys:
            arrive(yrecv.at[k, yy, part], y_r.at[k, yy, p])
            g = g + yrecv[k, yy, part].astype(F32)
        return g

    def cap_ready(k):
        for xx in xs:
            xsend[k * X + xx] = cap_part(k, xx).astype(BF)

    def clip_ready(k):
        for yy in ys:
            ysend[k, yy] = clip_both(k, yy).astype(BF)

    def issue_x(s):
        k, part = (zo if s < NP else zr), pl.ds(s % NP * H, H)
        for xx in xs:
            send(xsend.at[k * X + xx, part], xrecv.at[k * X + x, part], x_r.at[k * X + x, s % NP], dev(y, xx, c, z))

    def issue_y(s):
        k, part = (zo if s < NP else zr), pl.ds(s % NP * H, H)
        for yy in ys:
            send(ysend.at[k, yy, part], yrecv.at[k, y, part], y_r.at[k, y, s % NP], dev(yy, x, c, z))

    def issue(s):
        if s >= WS:
            settle(*waves[s - WS])
        first = len(sent)
        issue_x(s)
        issue_y(s)
        waves.append((first, len(sent)))

    def landed(s):
        p = s % NP
        part = pl.ds(p * H, H)
        if s < NP:
            cap_on(zo, p, None)
            zcsend[part] = clip_own(zo, p).astype(BF)
            send(zcsend.at[part], zcrecv.at[part], zc_r.at[p], dev(y, x, c, zc))
        else:
            cap_on(zr, p, passer)
            yacc[zr, y, part] = clip_own(zr, p)

    for yy in ys:
        scores(zo, zo, yy)
        scores(zr, zo, yy)
        clip_part(zo, yy)
    scores(zo, zo, y)
    for yy in range(Y):
        scores(zo, zr, yy)
    cap_ready(zo)
    waves = []
    clip_ready(zo)
    issue(0)
    scores(zr, zo, y)
    for yy in range(Y):
        scores(zr, zr, yy)
    issue(1)
    send(loss.at[sib], lcrecv, l_r.at[0], dev(y, x, sib, z))
    capacc[zo] = cap_part(zo, x)
    clip_part(zo, y)
    if NP > 2:
        issue(2)
    for yy in ys:
        clip_part(zr, yy)
    yacc[zo, y] = clip_both(zo, y)
    if NP > 2:
        landed(0)
        issue(3)
    cap_ready(zr)
    if NP > 2:
        landed(1)
    clip_ready(zr)
    issue(NP)
    arrive(lcrecv, l_r.at[0])
    loss[c] = loss[c] + lcrecv[...]
    for yy in ys:
        send(loss.at[c, yy], lyrecv.at[y], l_r.at[1 + y], dev(yy, x, c, z))
    clip_part(zr, y)
    landed(NP - 2)
    issue(NP + 1)
    capacc[zr] = cap_part(zr, x)
    landed(NP - 1)
    if NP > 2:
        issue(6)
    yacc[zr, y] = clip_both(zr, y)
    landed(NP)
    if NP > 2:
        issue(7)
        landed(5)
    for yy in ys:
        arrive(lyrecv.at[yy], l_r.at[1 + yy])
        loss[c, y] = loss[c, y] + lyrecv[yy]
    send(loss.at[c, y, zo], lzrecv, l_r.at[1 + Y], dev(y, x, c, zc))
    for s in range(2 * NP - 2 if NP > 2 else 3, 2 * NP):
        landed(s)

    for p in range(NP):
        arrive(zcrecv.at[pl.ds(p * H, H)], zc_r.at[p])
    clip_out[...] = yacc[zr, y] + zcrecv[...].astype(F32)
    arrive(lzrecv, l_r.at[1 + Y])
    loss_out[...] = loss[c, y, zr] + lzrecv[...]
    for j in range(2):
        plane = z // 2 + 2 * j

        @pl.when(plane == z)
        def _():
            cap_out[j] = capacc[zr]

        @pl.when(plane != z)
        def _():
            for p in range(NP):
                arrive(zrecv.at[j, pl.ds(p * H, H)], z_r.at[j, p])
            cap_out[j] = zrecv[j].astype(F32)

    settle(0)


def finish(clip_ref, cap_ref, clip_sum, cap_sum, loss_sum, clip_out, cap_out, loss_out):
    clip_out[...] = pull_back(clip_ref[...], clip_sum[...])
    cap_out[...] = pull_back(cap_ref[...], cap_sum[0] + cap_sum[1])
    loss_out[...] = loss_sum[...]


def local(Y, X, NZ, clip_embed, caption_embed, positive):
    R, D = clip_embed.shape
    ncl, ncap = 4 * Y, 2 * X
    V = pltpu.VMEM
    dma = pltpu.SemaphoreType.DMA
    scratch = [
        V((ncl * R, D), BF), V((ncap * R, D), BF), V((R, D), BF),
        V((2, Y, 2, 1, R), jnp.int32), V((ncap * R, ncl * R), BF), V((2, Y, 2, 1, R), F32),
        V((2, R, D), F32), V((ncap, R, D), BF), V((ncap, R, D), BF), V((2, R, D), BF), V((2, R, D), BF),
        V((2, Y, R, D), BF), V((2, Y, R, D), BF), V((Y, 2, 1, R), F32),
        V((2 * R, D), F32), V((2, Y, R, D), F32), V((2, Y, R, D), BF), V((2, Y, R, D), BF), V((Y, 2, 1, R), F32),
        V((R, D), BF), V((R, D), BF), V((1, R), F32),
        dma((32 + 32 * (X + Y),)), dma((ncl, NG)), dma((2 + Y,)), dma((ncap, NG)), dma((ncap, NP)), dma((2, NP)),
        dma((2, Y)), dma((2, Y, NP)), dma((NP,)), dma((2 + Y,)),
    ]
    vm = pl.BlockSpec(memory_space=V)
    sums = pl.pallas_call(
        functools.partial(kernel, Y, X, NZ),
        out_shape=(jax.ShapeDtypeStruct((R, D), F32), jax.ShapeDtypeStruct((2, R, D), F32),
                   jax.ShapeDtypeStruct((1, R), F32)),
        in_specs=[vm] * 3, out_specs=(vm,) * 3, scratch_shapes=scratch,
        compiler_params=pltpu.CompilerParams(
            collective_id=0, has_side_effects=True, vmem_limit_bytes=56 * 1024 * 1024),
    )(clip_embed, caption_embed, positive.reshape(1, 1, R))
    clip_grad, cap_grad, loss = pl.pallas_call(
        finish,
        out_shape=(jax.ShapeDtypeStruct((R, D), F32), jax.ShapeDtypeStruct((R, D), F32),
                   jax.ShapeDtypeStruct((1, R), F32)),
        in_specs=[vm] * 5, out_specs=(vm,) * 3,
    )(clip_embed, caption_embed, *sums)
    return clip_grad, cap_grad, loss.reshape(R)


def solution(mesh):
    n_dp, n_blk = mesh.shape["dp"], mesh.shape["blk"]
    assert n_blk == 4 and n_dp % 2 == 0
    plane = n_dp // 2
    Y = max(d for d in range(1, plane + 1) if plane % d == 0 and d * d <= plane)
    X = plane // Y
    specs = (P(("dp", "blk"), None), P(("dp", "blk"), None), P(("dp", "blk")))
    return jax.shard_map(functools.partial(local, Y, X, n_blk), mesh=mesh, in_specs=specs,
                         out_specs=specs, check_vma=False)
```

```python
import functools

import jax
import jax.numpy as jnp
from jax import lax
from jax.experimental import pallas as pl
from jax.experimental.pallas import tpu as pltpu
from jax.sharding import PartitionSpec as P

TEMP = 30.0
BIAS = -8.0
EPS = 1e-06
MESH = pl.DeviceIdType.MESH
BF = jnp.bfloat16
F32 = jnp.float32
NG = 4
NP = 4
WS = 3
WZ = 9


def unit_rows(embed):
    values = embed.astype(F32)
    scale = jnp.sqrt(jnp.sum(values * values, axis=1, keepdims=True) + EPS)
    return values / scale, scale


def pull_back(embed, grad_unit):
    unit_f, scale = unit_rows(embed)
    inner = jnp.sum(unit_f * grad_unit, axis=1, keepdims=True)
    return (grad_unit - unit_f * inner) / scale


def kernel(Y, X, NZ, clip_ref, cap_ref, pos_ref, clip_out, cap_out, loss_out,
           clips, caps, capown, pos, pt, loss, capacc, xsend, xrecv, zsend, zrecv,
           csend, crecv, lcrecv, acc, yacc, ysend, yrecv, lyrecv, zcsend, zcrecv, lzrecv,
           ssem, clip_r, pos_r, cap_r, x_r, z_r, c_r, y_r, zc_r, l_r):
    R, D = clip_ref.shape
    H, HG = R // NP, R // NG
    dp = lax.axis_index("dp")
    z = lax.axis_index("blk")
    c = dp % 2
    x = (dp // 2) % X
    y = dp // (2 * X)
    sib = 1 - c
    zr = z % 2
    zo = 1 - zr
    zc = z + 1 - 2 * zr

    def dev(yy, xx, cc, zz):
        return ((yy * X + xx) * 2 + cc, zz)

    def rows(slot, n=1):
        return pl.ds(pl.multiple_of(slot * R, R), n * R)

    def piece(slot, p):
        return pl.ds(pl.multiple_of(slot * R + p * HG, HG), HG)

    def slot_of(cc, yy, k):
        return (k * Y + yy) * 2 + cc

    count = [0]
    sent = []

    def send(src, dst, rsem, where, cond=None):
        copy = pltpu.make_async_remote_copy(
            src_ref=src, dst_ref=dst, send_sem=ssem.at[count[0]], recv_sem=rsem,
            device_id=where, device_id_type=MESH)
        count[0] += 1
        sent.append((copy, cond))
        if cond is None:
            copy.start()
        else:
            pl.when(cond)(copy.start)

    done = set()

    def settle(first, last=None):
        for i in range(first, len(sent) if last is None else last):
            if i in done:
                continue
            done.add(i)
            copy, cond = sent[i]
            if cond is None:
                copy.wait_send()
            else:
                pl.when(cond)(copy.wait_send)

    def arrive(dst, rsem):
        pltpu.make_async_remote_copy(
            src_ref=dst, dst_ref=dst, send_sem=ssem.at[0], recv_sem=rsem,
            device_id=dev(y, x, sib, z), device_id_type=MESH).wait_recv()

    ys = [(y + d) % Y for d in range(1, Y)]
    xs = [(x + d) % X for d in range(1, X)]
    peers = [dev(y, x, c, (z + d) % NZ) for d in range(1, NZ)]
    peers += [dev(yy, x, c, z) for yy in ys] + [dev(y, xx, c, z) for xx in xs]
    peers += [dev(y, x, sib, z)]
    barrier = pltpu.get_barrier_semaphore()
    for peer in peers:
        pl.semaphore_signal(barrier, inc=1, device_id=peer, device_id_type=MESH)

    mine = slot_of(c, y, zr)
    other = slot_of(c, y, zo)
    clips[rows(mine), :] = unit_rows(clip_ref[...])[0].astype(BF)
    capown[...] = unit_rows(cap_ref[...])[0].astype(BF)
    pos[c, y, zr] = pos_ref[0]
    pl.semaphore_wait(barrier, len(peers))

    owner = 3 * zr == z
    passer = jnp.logical_not(owner)
    zmarks = []

    def gather_z(p):
        if p >= WZ:
            settle(*zmarks[p - WZ])
        begin = len(sent)
        part = clips.at[piece(mine, p)]
        send(part, part, clip_r.at[mine, p], dev(y, x, c, zc))
        for j in range(2):
            to = z // 2 + 2 * j
            slot = zr * X + x
            send(capown.at[pl.ds(p * HG, HG)], caps.at[piece(slot, p)], cap_r.at[slot, p],
                 dev(y, x, c, to), to != z)
        zmarks.append((begin, len(sent)))

    for p in range(min(WZ, NG)):
        gather_z(p)
    send(pos.at[c, y, zr], pos.at[c, y, zr], pos_r.at[0], dev(y, x, c, zc))
    whole = clips.at[rows(mine)]
    for yy in ys:
        send(whole, whole, clip_r.at[mine, 0], dev(yy, x, c, z))
    send(whole, whole, clip_r.at[mine, 0], dev(y, x, sib, z))
    near, far = zr * X + x, zo * X + x

    @pl.when(owner)
    def _():
        caps[rows(near), :] = capown[...]

    for p in range(NG):
        part = caps.at[piece(near, p)]
        for xx in xs:
            send(part, part, cap_r.at[near, p], dev(y, xx, c, z), owner)
    for p in range(WZ, NG):
        gather_z(p)
    for p in range(NG):
        part = clips.at[piece(other, p)]
        arrive(part, clip_r.at[other, p])
        for yy in ys:
            send(part, part, clip_r.at[other, p], dev(yy, x, c, z))
        part = caps.at[piece(far, p)]
        arrive(part, cap_r.at[far, p])
        for xx in xs:
            send(part, part, cap_r.at[far, p], dev(y, xx, c, z))
        part = caps.at[piece(near, p)]

        @pl.when(passer)
        def _():
            arrive(part, cap_r.at[near, p])

        for xx in xs:
            send(part, part, cap_r.at[near, p], dev(y, xx, c, z), passer)
    whole = clips.at[rows(other)]
    send(whole, whole, clip_r.at[other, 0], dev(y, x, sib, z))
    arrive(pos.at[c, y, zo], pos_r.at[0])
    for yy in ys:
        send(pos.at[c, y], pos.at[c, y], pos_r.at[1 + y], dev(yy, x, c, z))
    for yy in ys:
        slot = slot_of(c, yy, zr)
        whole = clips.at[rows(slot)]
        arrive(whole, clip_r.at[slot, 0])
        send(whole, whole, clip_r.at[slot, 0], dev(y, x, sib, z))
    for yy in ys:
        arrive(pos.at[c, yy], pos_r.at[1 + yy])
    send(pos.at[c], pos.at[c], pos_r.at[1 + Y], dev(y, x, sib, z))
    for yy in ys:
        slot = slot_of(c, yy, zo)
        for p in range(NG):
            arrive(clips.at[piece(slot, p)], clip_r.at[slot, p])
        whole = clips.at[rows(slot)]
        send(whole, whole, clip_r.at[slot, 0], dev(y, x, sib, z))
    for k in range(2):
        for xx in xs:
            slot = k * X + xx
            for p in range(NG):
                arrive(caps.at[piece(slot, p)], cap_r.at[slot, p])
    for yy in range(Y):
        for k in range(2):
            slot = slot_of(sib, yy, k)
            arrive(clips.at[rows(slot)], clip_r.at[slot, 0])
    arrive(pos.at[sib], pos_r.at[1 + Y])

    half = X * R
    tile = lax.broadcasted_iota(jnp.int32, (half, 1), 0)
    cap_dev = (y * X + tile // R) * 2 + c

    def scores(k, kk, yy):
        b = kk * Y + yy
        cols = pl.ds(pl.multiple_of(b * 2 * R, 2 * R), 2 * R)
        sel = pl.ds(pl.multiple_of(k * half, half), half)
        dots = lax.dot_general(caps[sel, :], clips[cols, :], (((1,), (1,)), ((), ())),
                               preferred_element_type=F32)
        logits = TEMP * dots + BIAS
        ids = (cap_dev * NZ + 2 * zr + k) * R + tile % R
        target = jnp.concatenate([pos[0, yy, kk], pos[1, yy, kk]], axis=1)
        hit = ids == target
        t = jnp.where(hit, -logits, logits)
        a = jnp.exp(-jnp.abs(t))
        soft = jnp.maximum(t, 0.0) + jnp.log1p(a)
        sig = jnp.where(t >= 0.0, 1.0, a) / (1.0 + a)
        pt[sel, cols] = jnp.where(hit, -sig, sig).astype(BF)
        part = jnp.sum(soft, axis=0, keepdims=True)
        for m in range(2):
            loss[m, yy, kk] = loss[m, yy, kk] + part[:, m * R:(m + 1) * R]

    loss[...] = jnp.zeros_like(loss)

    def cap_part(k, xx):
        return TEMP * jnp.dot(pt[rows(k * X + xx), :], clips[...], preferred_element_type=F32)

    def clip_part(k, yy):
        both = pl.ds(pl.multiple_of((k * Y + yy) * 2 * R, 2 * R), 2 * R)
        acc[...] = TEMP * lax.dot_general(pt[:, both], caps[...], (((0,), (0,)), ((), ())),
                                          preferred_element_type=F32)
        csend[k, yy] = acc[rows(sib), :].astype(BF)
        send(csend.at[k, yy], crecv.at[k, yy], c_r.at[k, yy], dev(y, x, sib, z))
        yacc[k, yy] = acc[rows(c), :]

    def clip_both(k, yy):
        arrive(crecv.at[k, yy], c_r.at[k, yy])
        return yacc[k, yy] + crecv[k, yy].astype(F32)

    def cap_on(k, p, cond):
        part = pl.ds(p * H, H)
        g = capacc[k, part]
        for xx in xs:
            arrive(xrecv.at[k * X + xx, part], x_r.at[k * X + xx, p])
            g = g + xrecv[k * X + xx, part].astype(F32)
        capacc[k, part] = g
        zsend[k, part] = g.astype(BF)
        send(zsend.at[k, part], zrecv.at[z // 2, part], z_r.at[z // 2, p], dev(y, x, c, 2 * zr + k), cond)

    def clip_own(k, p):
        part = pl.ds(p * H, H)
        g = yacc[k, y, part]
        for yy in ys:
            arrive(yrecv.at[k, yy, part], y_r.at[k, yy, p])
            g = g + yrecv[k, yy, part].astype(F32)
        return g

    def cap_ready(k):
        for xx in xs:
            xsend[k * X + xx] = cap_part(k, xx).astype(BF)

    def clip_ready(k):
        for yy in ys:
            ysend[k, yy] = clip_both(k, yy).astype(BF)

    def issue_x(s):
        k, part = (zo if s < NP else zr), pl.ds(s % NP * H, H)
        for xx in xs:
            send(xsend.at[k * X + xx, part], xrecv.at[k * X + x, part], x_r.at[k * X + x, s % NP], dev(y, xx, c, z))

    def issue_y(s):
        k, part = (zo if s < NP else zr), pl.ds(s % NP * H, H)
        for yy in ys:
            send(ysend.at[k, yy, part], yrecv.at[k, y, part], y_r.at[k, y, s % NP], dev(yy, x, c, z))

    def issue(s):
        if s >= WS:
            settle(*waves[s - WS])
        first = len(sent)
        issue_x(s)
        issue_y(s)
        waves.append((first, len(sent)))

    def landed(s):
        p = s % NP
        part = pl.ds(p * H, H)
        if s < NP:
            cap_on(zo, p, None)
            zcsend[part] = clip_own(zo, p).astype(BF)
            send(zcsend.at[part], zcrecv.at[part], zc_r.at[p], dev(y, x, c, zc))
        else:
            cap_on(zr, p, passer)
            yacc[zr, y, part] = clip_own(zr, p)

    for yy in ys:
        scores(zo, zo, yy)
        scores(zr, zo, yy)
        clip_part(zo, yy)
    scores(zo, zo, y)
    for yy in range(Y):
        scores(zo, zr, yy)
    cap_ready(zo)
    waves = []
    clip_ready(zo)
    issue(0)
    scores(zr, zo, y)
    for yy in range(Y):
        scores(zr, zr, yy)
    issue(1)
    send(loss.at[sib], lcrecv, l_r.at[0], dev(y, x, sib, z))
    capacc[zo] = cap_part(zo, x)
    clip_part(zo, y)
    if NP > 2:
        issue(2)
    for yy in ys:
        clip_part(zr, yy)
    yacc[zo, y] = clip_both(zo, y)
    if NP > 2:
        landed(0)
        issue(3)
    cap_ready(zr)
    if NP > 2:
        landed(1)
    clip_ready(zr)
    issue(NP)
    arrive(lcrecv, l_r.at[0])
    loss[c] = loss[c] + lcrecv[...]
    for yy in ys:
        send(loss.at[c, yy], lyrecv.at[y], l_r.at[1 + y], dev(yy, x, c, z))
    clip_part(zr, y)
    landed(NP - 2)
    issue(NP + 1)
    capacc[zr] = cap_part(zr, x)
    landed(NP - 1)
    if NP > 2:
        issue(6)
    yacc[zr, y] = clip_both(zr, y)
    landed(NP)
    if NP > 2:
        issue(7)
        landed(5)
    for yy in ys:
        arrive(lyrecv.at[yy], l_r.at[1 + yy])
        loss[c, y] = loss[c, y] + lyrecv[yy]
    send(loss.at[c, y, zo], lzrecv, l_r.at[1 + Y], dev(y, x, c, zc))
    for s in range(2 * NP - 2 if NP > 2 else 3, 2 * NP):
        landed(s)

    for p in range(NP):
        arrive(zcrecv.at[pl.ds(p * H, H)], zc_r.at[p])
    clip_out[...] = yacc[zr, y] + zcrecv[...].astype(F32)
    arrive(lzrecv, l_r.at[1 + Y])
    loss_out[...] = loss[c, y, zr] + lzrecv[...]
    for j in range(2):
        plane = z // 2 + 2 * j

        @pl.when(plane == z)
        def _():
            cap_out[...] = capacc[zr] if j == 0 else cap_out[...] + capacc[zr]

        @pl.when(plane != z)
        def _():
            for p in range(NP):
                arrive(zrecv.at[j, pl.ds(p * H, H)], z_r.at[j, p])
            cap_out[...] = zrecv[j].astype(F32) if j == 0 else cap_out[...] + zrecv[j].astype(F32)

    settle(0)


def finish(clip_ref, cap_ref, clip_sum, cap_sum, loss_sum, clip_out, cap_out, loss_out):
    clip_out[...] = pull_back(clip_ref[...], clip_sum[...])
    cap_out[...] = pull_back(cap_ref[...], cap_sum[...])
    loss_out[...] = loss_sum[...]


def local(Y, X, NZ, clip_embed, caption_embed, positive):
    R, D = clip_embed.shape
    ncl, ncap = 4 * Y, 2 * X
    V = pltpu.VMEM
    dma = pltpu.SemaphoreType.DMA
    scratch = [
        V((ncl * R, D), BF), V((ncap * R, D), BF), V((R, D), BF),
        V((2, Y, 2, 1, R), jnp.int32), V((ncap * R, ncl * R), BF), V((2, Y, 2, 1, R), F32),
        V((2, R, D), F32), V((ncap, R, D), BF), V((ncap, R, D), BF), V((2, R, D), BF), V((2, R, D), BF),
        V((2, Y, R, D), BF), V((2, Y, R, D), BF), V((Y, 2, 1, R), F32),
        V((2 * R, D), F32), V((2, Y, R, D), F32), V((2, Y, R, D), BF), V((2, Y, R, D), BF), V((Y, 2, 1, R), F32),
        V((R, D), BF), V((R, D), BF), V((1, R), F32),
        dma((32 + 32 * (X + Y),)), dma((ncl, NG)), dma((2 + Y,)), dma((ncap, NG)), dma((ncap, NP)), dma((2, NP)),
        dma((2, Y)), dma((2, Y, NP)), dma((NP,)), dma((2 + Y,)),
    ]
    vm = pl.BlockSpec(memory_space=V)
    sums = pl.pallas_call(
        functools.partial(kernel, Y, X, NZ),
        out_shape=(jax.ShapeDtypeStruct((R, D), F32), jax.ShapeDtypeStruct((R, D), F32),
                   jax.ShapeDtypeStruct((1, R), F32)),
        in_specs=[vm] * 3, out_specs=(vm,) * 3, scratch_shapes=scratch,
        compiler_params=pltpu.CompilerParams(
            collective_id=0, has_side_effects=True, vmem_limit_bytes=56 * 1024 * 1024),
    )(clip_embed, caption_embed, positive.reshape(1, 1, R))
    clip_grad, cap_grad, loss = pl.pallas_call(
        finish,
        out_shape=(jax.ShapeDtypeStruct((R, D), F32), jax.ShapeDtypeStruct((R, D), F32),
                   jax.ShapeDtypeStruct((1, R), F32)),
        in_specs=[vm] * 5, out_specs=(vm,) * 3,
    )(clip_embed, caption_embed, *sums)
    return clip_grad, cap_grad, loss.reshape(R)


def solution(mesh):
    n_dp, n_blk = mesh.shape["dp"], mesh.shape["blk"]
    assert n_blk == 4 and n_dp % 2 == 0
    plane = n_dp // 2
    Y = max(d for d in range(1, plane + 1) if plane % d == 0 and d * d <= plane)
    X = plane // Y
    specs = (P(("dp", "blk"), None), P(("dp", "blk"), None), P(("dp", "blk")))
    return jax.shard_map(functools.partial(local, Y, X, n_blk), mesh=mesh, in_specs=specs,
                         out_specs=specs, check_vma=False)
```
